32 devices in a mesh: rep: 2 (over y), req: 4 (over x, core), tp: 4 (over z).
Axes of the slice: x: 2, y: 2, z: 4, core: 2. Of those that a mesh axis runs over, the one named last changes fastest.
Arguments:
- hidden: bfloat16 [64, 8192], P(('rep', 'req'), 'tp'), parts along dimension 0, may hold values from -6 to 6
- value_projection_weight: bfloat16 [8192, 1024], P('tp'), may hold values from -0.0625 to 0.0625
- adapter_down_weight: bfloat16 [4096, 16, 8192], P(('rep', 'req'), None, 'tp'), parts along dimension 0, may hold values from -0.0625 to 0.0625
- adapter_up_weight: bfloat16 [4096, 16, 1024], P(('rep', 'req'), None, 'tp'), parts along dimension 0, may hold values from -1.5 to 1.5
- adapter_store_row: int32 [4096], P('rep'), parts along dimension 0, may hold values from 0 to 2047, as said below
- request_group_adapters: int32 [64], P(('rep', 'req')), parts along dimension 0, may hold values from 0 to 2047, as said below
- row_list_entry: int32 [64, 1], P(('rep', 'req')), parts along dimension 0, may hold values from 0 to 7
- cache_length: int32 [64], P(('rep', 'req')), parts along dimension 0, may hold values from 2 to 512, as said below
- query: bfloat16 [64, 8192], P(('rep', 'req')), parts along dimension 0, may hold values from -6 to 6
- cached_key_rows: bfloat16 [64, 512, 1024], P(('rep', 'req'), 'tp'), parts along dimension 0, may hold values from -6 to 6
- cached_value_rows: bfloat16 [64, 512, 1024], P(('rep', 'req'), 'tp'), parts along dimension 0, may hold values from -6 to 6
- new_token_keys: bfloat16 [64, 1024], P(('rep', 'req')), parts along dimension 0, may hold values from -6 to 6
Outputs:
- value_new: bfloat16 [64, 1024], P(('rep', 'req')), parts along dimension 0
- attention_out: bfloat16 [64, 8192], P(('rep', 'req'), 'tp'), parts along dimension 0
The draws below stay inside these ranges and needn't reach their ends.
There are 2 independent parts, one for each index of `rep`. The reference program is written for one: setup_inputs(seed, part) draws one part's arguments, and reference() takes and returns one part's arrays. A program takes and returns all parts, laid end to end along the dimension named above; an argument that names none is the same for every part. Nothing has to cross between parts.
Inputs may be any that keep to these rules, and one draw needn't show every extreme that they name: A permutation: adapter a lives at store row adapter_store_row[a] of adapter_down_weight and adapter_up_weight, that is in the store of request group adapter_store_row[a] // 512. `request_group_adapters`: each group's 8 entries are distinct adapter ids; at most 2 of one group's entries live in one request group's store, and in every group some store holds exactly 2 of them. `row_list_entry`: an index into the row's own group's list. `cache_length`: some row has a full cache.
All inputs are finite; a program needn't handle non-finite values.
Results may differ from the reference program's by a relative error of at most 0.0041.
Values may be sent and summed in bfloat16 or wider, within the bound.
A program may use at most 128 MiB of HBM per device.

```python
import jax
import jax.numpy as jnp
from jax import lax

MODEL_WIDTH = 8192
HEADS = 64
KV_HEADS = 8
HD = 128
ADAPTER_RANK = 16
ADAPTER_TOTAL = 2048
SEG = 8
CAP = 2
ROW_GRP = 8
LEN = 512
ROWS = 32
KEY_VALUE_WIDTH = 1024
N_REQ = 4
N_TP = 4


def placement_table(key):
    return jax.random.permutation(jax.random.fold_in(key, 7), ADAPTER_TOTAL).astype(jnp.int32)


def length_table(key):
    inner = jax.random.fold_in(key, 9)
    first, second = jax.random.split(inner)
    lengths = jax.random.randint(first, (ROWS,), 2, LEN + 1)
    longest = jax.random.randint(second, (), 0, ROWS)
    return lengths.at[longest].set(LEN).astype(jnp.int32)


def draw_adapter_store_row(key, part):
    return placement_table(key)


def group_list(key, inverse):
    store_row_index = ADAPTER_TOTAL // N_REQ
    first, second, third, fourth = jax.random.split(key, 4)
    favoured = jax.random.randint(first, (), 0, N_REQ)
    pool = jnp.arange(N_REQ * CAP, dtype=jnp.int32) // CAP
    ranking = jax.random.permutation(second, N_REQ * CAP).astype(jnp.int32)
    priority = jnp.where(pool == favoured, -1, ranking)
    ordering = jnp.argsort(priority, stable=True)
    owners = pool[ordering][:SEG]
    earlier = jnp.arange(SEG)[:, None] > jnp.arange(SEG)[None, :]
    counted = jnp.sum((owners[:, None] == owners[None, :]) & earlier, axis=1)
    shuffles = jax.vmap(lambda inner: jax.random.permutation(inner, store_row_index))(jax.random.split(third, N_REQ))
    slot_index = shuffles[owners, counted]
    chosen_ids = inverse[owners * store_row_index + slot_index]
    return chosen_ids[jax.random.permutation(fourth, SEG)]


def draw_request_group_adapters(key, part):
    inverse = jnp.argsort(placement_table(key)).astype(jnp.int32)
    key = jax.random.fold_in(key, 11)
    lists = jax.vmap(lambda inner: group_list(inner, inverse))(jax.random.split(key, N_REQ))
    return lists.reshape(N_REQ * SEG).astype(jnp.int32)


def draw_cache_length(key, part):
    lengths = length_table(key)
    return lengths


def draw_query(key, part):
    key = jax.random.fold_in(key, 3)
    array_shape = (ROWS, HEADS * HD)
    values = jnp.clip(jax.random.normal(key, array_shape, jnp.float32), -6.0, 6.0)
    return values.astype(jnp.bfloat16)


def draw_cached_key_rows(key, part):
    key = jax.random.fold_in(key, 5)
    array_shape = (ROWS, LEN, KV_HEADS * HD)
    values = jnp.clip(jax.random.normal(key, array_shape, jnp.float32), -6.0, 6.0)
    return values.astype(jnp.bfloat16)


def block_levels(rng, dims, cuts, least, high):
    def one(dim, shards_of):
        draws = jax.random.uniform(jax.random.fold_in(jax.random.fold_in(rng, 6), dim), (shards_of,), jnp.float32, least / len(cuts), high / len(cuts))
        return jnp.repeat(jnp.exp(draws), dims[dim] // shards_of).reshape((-1,) + (1,) * (len(dims) - dim - 1))

    factor_of = one(*cuts[0])
    for cut in cuts[1:]:
        factor_of = factor_of * one(*cut)
    return factor_of


def picks_of(rng, rows, amount, top, lift):
    order = jax.random.permutation(jax.random.fold_in(rng, 1), amount)
    pull = order
    for power in range(3):
        pull = pull * pull // amount
    pull = pull * lift // amount
    lots = jax.random.randint(jax.random.fold_in(rng, 2), (rows, amount), 0, 4096) + pull
    holders = jax.random.permutation(jax.random.fold_in(rng, 3), rows)[jnp.arange(amount) % rows]
    lots = jnp.where(jnp.arange(rows)[:, None] == holders[None, :], 1 << 14, lots)
    score = lots * amount + jnp.arange(amount)
    return lax.top_k(score.astype(jnp.int32), top)[1].astype(jnp.int32)


def bell_draw(stream_key, dims, spread, reach, cuts=(), kind=jnp.bfloat16):
    loudness = block_levels(stream_key, dims, cuts, -0.22, 0.18) if cuts else 1.0
    result = jax.random.normal(stream_key, dims, jnp.float32) * spread * loudness
    return jnp.minimum(jnp.maximum(result, -reach), reach).astype(kind)


def setup_inputs(seed: int = 0, part: int = 0) -> dict:
    seeds = jax.random.split(jax.random.key(seed), 13)
    part_keys = jax.random.split(jax.random.fold_in(seeds[12], part), 13)
    return {
        "hidden": bell_draw(part_keys[0], (ROWS, MODEL_WIDTH), 1.0, 6.0, ((0, 4), (1, 4))),
        "value_projection_weight": bell_draw(seeds[1], (MODEL_WIDTH, KEY_VALUE_WIDTH), MODEL_WIDTH ** -0.5, 0.0625, ((0, 4),)),
        "adapter_down_weight": bell_draw(part_keys[2], (ADAPTER_TOTAL, ADAPTER_RANK, MODEL_WIDTH), MODEL_WIDTH ** -0.5, 0.0625, ((0, 4), (2, 4))),
        "adapter_up_weight": bell_draw(part_keys[3], (ADAPTER_TOTAL, ADAPTER_RANK, KEY_VALUE_WIDTH), ADAPTER_RANK ** -0.5, 1.5, ((0, 4), (2, 4))),
        "adapter_store_row": draw_adapter_store_row(jax.random.fold_in(jax.random.fold_in(seeds[12], part), 71), part),
        "request_group_adapters": draw_request_group_adapters(jax.random.fold_in(jax.random.fold_in(seeds[12], part), 71), part),
        "row_list_entry": picks_of(part_keys[6], ROWS, SEG, 1, 2048),
        "cache_length": draw_cache_length(jax.random.fold_in(jax.random.fold_in(seeds[12], part), 71), part),
        "query": draw_query(jax.random.fold_in(jax.random.fold_in(seeds[12], part), 71), part),
        "cached_key_rows": draw_cached_key_rows(jax.random.fold_in(jax.random.fold_in(seeds[12], part), 71), part),
        "cached_value_rows": bell_draw(part_keys[10], (ROWS, LEN, KEY_VALUE_WIDTH), 1.0, 6.0, ((0, 4), (1, 4))),
        "new_token_keys": bell_draw(part_keys[11], (ROWS, KEY_VALUE_WIDTH), 1.0, 6.0, ((0, 4),)),
    }


masked_score = -1e30


def reference(hidden, value_projection_weight, adapter_down_weight, adapter_up_weight, adapter_store_row, request_group_adapters, row_list_entry, cache_length, query, cached_key_rows, cached_value_rows, new_token_keys):
    total_rows = hidden.shape[0]
    per_group = HEADS // KV_HEADS
    block_len = LEN // N_TP
    highest = lax.Precision.HIGHEST
    lists = request_group_adapters.reshape(N_REQ, SEG)
    picked = row_list_entry.reshape(N_REQ, ROW_GRP).astype(jnp.int32)
    row_ids = jnp.take_along_axis(lists, picked, axis=1).reshape(total_rows)
    row_store_index = adapter_store_row[row_ids]
    down_matrix_rows = adapter_down_weight[row_store_index].astype(jnp.float32)
    up_matrix_rows = adapter_up_weight[row_store_index].astype(jnp.float32)
    low_rank = jnp.einsum("rd,rkd->rk", hidden.astype(jnp.float32), down_matrix_rows, precision=highest)
    base_values = jnp.dot(hidden, value_projection_weight, preferred_element_type=jnp.float32)
    value_new = (base_values + jnp.einsum("rk,rkc->rc", low_rank, up_matrix_rows, precision=highest)).astype(jnp.bfloat16)
    queries = query.astype(jnp.float32).reshape(total_rows, KV_HEADS, per_group, HD)
    keys = cached_key_rows.astype(jnp.float32).reshape(total_rows, N_TP, block_len, KV_HEADS, HD)
    values = cached_value_rows.astype(jnp.float32).reshape(total_rows, N_TP, block_len, KV_HEADS, HD)
    scale_factor = HD ** -0.5
    scores = jnp.einsum("rkgd,rnlkd->rnkgl", queries, keys, precision=highest) * scale_factor
    positions = jnp.arange(LEN, dtype=jnp.int32).reshape(N_TP, block_len)
    valid = positions[None, :, None, None, :] < cache_length[:, None, None, None, None]
    scores = jnp.where(valid, scores, masked_score)
    block_max = jnp.max(scores, axis=4)
    probs = jnp.where(valid, jnp.exp(scores - block_max[..., None]), 0.0).astype(jnp.bfloat16)
    probs_wide = probs.astype(jnp.float32)
    block_den = jnp.sum(probs_wide, axis=4)
    block_acc = jnp.einsum("rnkgl,rnlkd->rnkgd", probs_wide, values, precision=highest)
    fresh_keys = new_token_keys.astype(jnp.float32).reshape(total_rows, KV_HEADS, HD)
    fresh_score = jnp.einsum("rkgd,rkd->rkg", queries, fresh_keys, precision=highest) * scale_factor
    peak = jnp.maximum(jnp.max(block_max, axis=1), fresh_score)
    weight_old = jnp.exp(block_max - peak[:, None])
    weight_new = jnp.exp(fresh_score - peak)
    fresh_value = value_new.astype(jnp.float32).reshape(total_rows, KV_HEADS, 1, HD)
    total_den = jnp.sum(block_den * weight_old, axis=1) + weight_new
    total_acc = jnp.sum(block_acc * weight_old[..., None], axis=1) + weight_new[..., None] * fresh_value
    attention_out = (total_acc / total_den[..., None]).reshape(total_rows, HEADS * HD).astype(jnp.bfloat16)
    return value_new, attention_out
```

```python
import functools

import jax
import jax.numpy as jnp
from jax import lax
from jax.experimental import pallas as pl
from jax.experimental.pallas import tpu as pltpu
from jax.sharding import PartitionSpec as P

HD = 128
ADAPTER_RANK = 16
CAP = 2
MASKED = -1e30
F32 = jnp.float32
BF16 = jnp.bfloat16
MESH = pl.DeviceIdType.MESH
VMEM = pl.BlockSpec(memory_space=pltpu.VMEM)
SMEM = pl.BlockSpec(memory_space=pltpu.SMEM)
ANY = pl.BlockSpec(memory_space=pl.ANY)


def dot_nt(a, b):
    return lax.dot_general(a, b, (((1,), (1,)), ((), ())), preferred_element_type=F32)


def request_kernel(groups, ids_ref, hidden_ref, ids_out, hidden_out, send_sems, recv_sems):
    me = lax.axis_index("req")
    half = hidden_ref.shape[1] // 2
    barrier = pltpu.get_barrier_semaphore()

    def greet(d, _):
        peer = lax.rem(me + d, groups)
        pl.semaphore_signal(barrier, inc=1, device_id={"req": peer}, device_id_type=MESH)
        return 0

    lax.fori_loop(1, groups, greet, 0)
    wide = hidden_ref[...].astype(F32)
    hidden_out[me] = jnp.concatenate([wide[:, :half], wide[:, half:]], axis=0).astype(BF16)
    ids_out[me] = ids_ref[...]
    pl.semaphore_wait(barrier, groups - 1)

    def copies(d):
        peer = lax.rem(me + d, groups)
        return [
            pltpu.make_async_remote_copy(
                src_ref=ref.at[me],
                dst_ref=ref.at[me],
                send_sem=send_sems.at[n, d],
                recv_sem=recv_sems.at[n, d],
                device_id={"req": peer},
                device_id_type=MESH,
            )
            for n, ref in enumerate((ids_out, hidden_out))
        ]

    def start(d, _):
        for copy in copies(d):
            copy.start()
        return 0

    def finish(d, _):
        for copy in copies(d):
            copy.wait()
        return 0

    lax.fori_loop(1, groups, start, 0)
    lax.fori_loop(1, groups, finish, 0)


def local_kernel(
    groups,
    parts,
    ids,
    table,
    lengths,
    hidden_all,
    hidden,
    query,
    new_keys,
    weight,
    down,
    up,
    keys,
    values,
    low_out,
    up_out,
    base_out,
    acc_out,
    stats_out,
    fresh_out,
    key_buf,
    value_buf,
    weight_buf,
    down_buf,
    slots,
    key_sems,
    value_sems,
    weight_sems,
    down_sems,
    up_sems,
):
    me = lax.axis_index("req")
    tp = lax.axis_index("tp")
    rows, depth = hidden.shape
    kv_width = new_keys.shape[1]
    kv_heads = kv_width // HD
    heads = query.shape[1] // HD
    per = heads // kv_heads
    here = heads // parts
    block = keys.shape[1]
    store = down.shape[0]
    entries = ids.shape[1]
    scale = HD ** (-0.5)

    chunks = key_sems.shape[0]
    wide = kv_width // chunks
    pieces = weight_sems.shape[0]
    tall = depth // pieces

    def key_copy(c):
        part = pl.ds(c * wide, wide)
        return pltpu.make_async_copy(keys.at[:, :, part], key_buf.at[:, :, part], key_sems.at[c])

    def value_copy(c):
        part = pl.ds(c * wide, wide)
        return pltpu.make_async_copy(
            values.at[:, :, part], value_buf.at[:, :, part], value_sems.at[c]
        )

    def weight_copy(c):
        part = pl.ds(c * tall, tall)
        return pltpu.make_async_copy(weight.at[part, :], weight_buf.at[part, :], weight_sems.at[c])

    def down_copy(place, slot):
        part = pl.ds(slot * ADAPTER_RANK, ADAPTER_RANK)
        return pltpu.make_async_copy(down.at[place], down_buf.at[part, :], down_sems.at[slot])

    def up_copy(place, slot):
        part = pl.ds(slot * ADAPTER_RANK, ADAPTER_RANK)
        return pltpu.make_async_copy(up.at[place], up_out.at[part, :], up_sems.at[slot])

    for c in range(chunks):
        key_copy(c).start()
        value_copy(c).start()
    for c in range(pieces):
        weight_copy(c).start()

    up_out[...] = jnp.zeros_like(up_out)
    counts = []
    for g in range(groups):
        count = jnp.int32(0)
        for e in range(entries):
            at = table[ids[g, e, 1]]
            mine = (at // store == me) & (count < CAP)
            slot = g * CAP + count
            slots[g * entries + e] = jnp.where(mine, slot, -1)

            @pl.when(mine)
            def _():
                down_copy(lax.rem(at, store), slot).start()
                up_copy(lax.rem(at, store), slot).start()

            count = count + mine.astype(jnp.int32)
        counts.append(count)

    lane = lax.broadcasted_iota(jnp.int32, (rows, 128), 1)
    sub = lax.broadcasted_iota(jnp.int32, (rows, block), 0)
    length = jnp.zeros((rows, block), jnp.int32)
    for r in range(rows):
        length = jnp.where(sub == r, lengths[r], length)
    position = tp * block + lax.broadcasted_iota(jnp.int32, (rows, block), 1)
    valid_one = (position < length).astype(jnp.int32)
    valid = jnp.concatenate([valid_one] * per, axis=0) > 0

    def own_row(width):
        shape = (per * rows, rows * width)
        row = lax.rem(lax.broadcasted_iota(jnp.int32, shape, 0), rows)
        col = lax.broadcasted_iota(jnp.int32, shape, 1) // width
        return jnp.where(row == col, 1.0, 0.0).astype(BF16)

    own_key = own_row(HD)
    lined = block % 128 == 0
    own_prob = own_key if block == HD else own_row(block) if lined else None
    row_of = lax.rem(lax.broadcasted_iota(jnp.int32, (per * rows, block), 0), rows)

    peaks = [jnp.zeros((rows, 128), F32) for _ in range(parts)]
    sums = [jnp.zeros((rows, 128), F32) for _ in range(parts)]
    for k in range(kv_heads):
        if (k * HD) % wide == 0:
            key_copy(k * HD // wide).wait()
            value_copy(k * HD // wide).wait()
        cols = slice(k * HD, (k + 1) * HD)
        q = jnp.concatenate(
            [
                query[:, (k * per + g) * HD : (k * per + g + 1) * HD].astype(F32)
                for g in range(per)
            ],
            axis=0,
        ).astype(BF16)
        q_wide = jnp.concatenate([q] * rows, axis=1) * own_key
        k_wide = jnp.concatenate([key_buf[r, :, cols] for r in range(rows)], axis=1)
        score = dot_nt(q_wide, k_wide) * scale
        score = jnp.where(valid, score, MASKED)
        peak = jnp.max(score, axis=1, keepdims=True)
        prob = jnp.where(valid, jnp.exp(score - peak), 0.0).astype(BF16)
        prob_f32 = prob.astype(F32)
        total = jnp.sum(prob_f32, axis=1, keepdims=True)
        if lined:
            p_wide = jnp.concatenate([prob] * rows, axis=1) * own_prob
            v_tall = value_buf[:, :, cols].reshape(rows * block, HD)
            acc = jnp.dot(p_wide, v_tall, preferred_element_type=F32)
        else:
            acc = jnp.zeros((per * rows, HD), F32)
            for r in range(rows):
                p_row = jnp.where(row_of == r, prob_f32, 0.0).astype(BF16)
                acc = acc + jnp.dot(p_row, value_buf[r, :, cols], preferred_element_type=F32)
        step = min(per, here)
        for c in range(per // step):
            first = k * per + c * step
            acc_out[first // here, (first % here) * rows : (first % here + step) * rows, :] = acc[
                c * step * rows : (c + 1) * step * rows
            ].astype(BF16)
        for g in range(per):
            head = k * per + g
            part = slice(g * rows, (g + 1) * rows)
            hit = lane == head % here
            peaks[head // here] = jnp.where(hit, peak[part], peaks[head // here])
            sums[head // here] = jnp.where(hit, total[part], sums[head // here])
    for p in range(parts):
        stats_out[p, :rows] = peaks[p]
        stats_out[p, rows:] = sums[p]

    fresh = jnp.zeros((rows, 128), F32)
    for j in range(here):
        head = tp * here + j
        q_at = pl.multiple_of(head * HD, HD)
        k_at = pl.multiple_of(head // per * HD, HD)
        both = query[:, pl.ds(q_at, HD)].astype(F32) * new_keys[:, pl.ds(k_at, HD)].astype(F32)
        fresh = jnp.where(lane == j, jnp.sum(both, axis=1, keepdims=True) * scale, fresh)
    fresh_out[...] = fresh

    base = jnp.zeros((rows, kv_width), F32)
    for c in range(pieces):
        weight_copy(c).wait()
        part = slice(c * tall, (c + 1) * tall)
        base = base + jnp.dot(hidden[:, part], weight_buf[part, :], preferred_element_type=F32)
    base_out[...] = base

    for g in range(groups):
        for c in range(CAP):

            @pl.when(counts[g] > c)
            def _():
                down_copy(0, g * CAP + c).wait()
                up_copy(0, g * CAP + c).wait()

    half = depth // 2
    width = low_out.shape[1]
    h_all = hidden_all[...].reshape(groups * 2 * rows, half)
    left = dot_nt(h_all, down_buf[:, :half])
    right = dot_nt(h_all, down_buf[:, half:])
    slot_lane = lax.broadcasted_iota(jnp.int32, (rows, width), 1) // ADAPTER_RANK
    slot_row = lax.broadcasted_iota(jnp.int32, (rows, width), 0)
    for g in range(groups):
        wanted = jnp.full((rows, width), -1, jnp.int32)
        for r in range(rows):
            wanted = jnp.where(slot_row == r, slots[g * entries + ids[g, r, 0]], wanted)
        top = g * 2 * rows
        low = left[top : top + rows] + right[top + rows : top + 2 * rows]
        low_out[g * rows : (g + 1) * rows] = jnp.where(wanted == slot_lane, low, 0.0)


def finish_kernel(
    groups,
    parts,
    low,
    up,
    base,
    acc,
    stats,
    fresh,
    value_out,
    attention_out,
    low_recv,
    base_recv,
    acc_recv,
    stats_recv,
    reply,
    reply_recv,
    value_heads,
    send_sems,
    recv_sems,
    reply_send,
    reply_recv_sems,
):
    me = lax.axis_index("req")
    tp = lax.axis_index("tp")
    rows, kv_width = base.shape
    kv_heads = kv_width // HD
    here = attention_out.shape[1] // HD
    per = here * parts // kv_heads
    columns = up.shape[1]
    total = groups * parts
    mine = me * parts + tp
    barrier = pltpu.get_barrier_semaphore()

    def member(o):
        at = lax.rem(mine + o, total)
        return at // parts, lax.rem(at, parts)

    def greet(o, _):
        peer_req, peer_tp = member(o)
        pl.semaphore_signal(
            barrier, inc=1, device_id={"req": peer_req, "tp": peer_tp}, device_id_type=MESH
        )
        return 0

    lax.fori_loop(1, total, greet, 0)
    low_recv[tp] = low[...]
    base_recv[tp] = base[...]
    stats_recv[tp] = stats[tp]
    acc_recv[tp] = acc[tp]
    pl.semaphore_wait(barrier, total - 1)

    def share(n, d):
        peer = lax.rem(tp + d, parts)
        source, landing = (
            lambda: (low, low_recv),
            lambda: (stats.at[peer], stats_recv),
            lambda: (base, base_recv),
            lambda: (acc.at[peer], acc_recv),
        )[n]()
        return pltpu.make_async_remote_copy(
            src_ref=source,
            dst_ref=landing.at[tp],
            send_sem=send_sems.at[n, d],
            recv_sem=recv_sems.at[n, d],
            device_id={"tp": peer},
            device_id_type=MESH,
        )

    def each(n, act):
        def step(d, _):
            act(share(n, d))
            return 0

        lax.fori_loop(1, parts, step, 0)

    for n in range(4):
        each(n, lambda copy: copy.start())
    each(0, lambda copy: copy.wait_recv())

    rank_sum = low_recv[0]
    for p in range(1, parts):
        rank_sum = rank_sum + low_recv[p]
    coarse = rank_sum.astype(BF16)
    fine = (rank_sum - coarse.astype(F32)).astype(BF16)
    term = jnp.dot(coarse, up[...], preferred_element_type=F32) + jnp.dot(
        fine, up[...], preferred_element_type=F32
    )
    for g in range(groups):
        reply[g] = term[g * rows : (g + 1) * rows]

    def reply_copy(o):
        peer_req, peer_tp = member(o)
        return pltpu.make_async_remote_copy(
            src_ref=reply.at[peer_req],
            dst_ref=reply_recv.at[me, tp],
            send_sem=reply_send.at[o],
            recv_sem=reply_recv_sems.at[o],
            device_id={"req": peer_req, "tp": peer_tp},
            device_id_type=MESH,
        )

    def reply_start(o, _):
        reply_copy(o).start()
        return 0

    lax.fori_loop(1, total, reply_start, 0)
    reply_recv[me, tp] = reply[me]

    for n in range(1, 4):
        each(n, lambda copy: copy.wait_recv())
    fresh_score = fresh[...]
    peak = fresh_score
    for p in range(parts):
        peak = jnp.maximum(peak, stats_recv[p, :rows])
    fresh_weight = jnp.exp(fresh_score - peak)
    weights = [jnp.exp(stats_recv[p, :rows] - peak) for p in range(parts)]
    den = fresh_weight
    for p in range(parts):
        den = den + weights[p] * stats_recv[p, rows:]
    inverse = 1.0 / den
    fresh_weight = fresh_weight * inverse
    weights = [weight * inverse for weight in weights]
    old = []
    for j in range(here):
        part = jnp.zeros((rows, HD), F32)
        for p in range(parts):
            block = acc_recv[p].astype(F32)[j * rows : (j + 1) * rows]
            part = part + weights[p][:, j : j + 1] * block
        old.append(part)

    base_sum = base_recv[0]
    for p in range(1, parts):
        base_sum = base_sum + base_recv[p]

    def reply_finish(o, _):
        reply_copy(o).wait_recv()
        return 0

    lax.fori_loop(1, total, reply_finish, 0)
    adapter = []
    for p in range(parts):
        piece = reply_recv[0, p]
        for g in range(1, groups):
            piece = piece + reply_recv[g, p]
        adapter.append(piece)
    value = (base_sum + jnp.concatenate(adapter, axis=1)).astype(BF16)
    value_out[...] = value
    value_f32 = value.astype(F32)
    for k in range(kv_heads):
        value_heads[k] = value_f32[:, k * HD : (k + 1) * HD]
    for j in range(here):
        fresh_value = value_heads[(tp * here + j) // per]
        out = old[j] + fresh_weight[:, j : j + 1] * fresh_value
        attention_out[:, j * HD : (j + 1) * HD] = out.astype(BF16)

    for n in range(4):
        each(n, lambda copy: copy.wait_send())

    def reply_sent(o, _):
        reply_copy(o).wait_send()
        return 0

    lax.fori_loop(1, total, reply_sent, 0)


def per_device(
    groups,
    parts,
    hidden,
    value_projection_weight,
    adapter_down_weight,
    adapter_up_weight,
    adapter_store_row,
    request_group_adapters,
    row_list_entry,
    cache_length,
    query,
    cached_key_rows,
    cached_value_rows,
    new_token_keys,
):
    rows, depth = hidden.shape
    kv_width = new_token_keys.shape[1]
    columns = adapter_up_weight.shape[2]
    heads = query.shape[1] // HD
    here = heads // parts
    block = cached_key_rows.shape[1]
    entries = request_group_adapters.shape[0]
    slot_rows = groups * CAP * ADAPTER_RANK
    total = groups * parts
    dma = pltpu.SemaphoreType.DMA
    shape = jax.ShapeDtypeStruct

    ids = jnp.concatenate([row_list_entry, request_group_adapters[:, None]], axis=1)
    ids = jnp.pad(ids, ((0, 0), (0, 126)))
    ids_all, hidden_all = pl.pallas_call(
        functools.partial(request_kernel, groups),
        out_shape=(
            shape((groups, entries, 128), jnp.int32),
            shape((groups, 2 * rows, depth // 2), BF16),
        ),
        in_specs=[VMEM] * 2,
        out_specs=(VMEM, VMEM),
        scratch_shapes=[dma((2, groups)), dma((2, groups))],
        compiler_params=pltpu.CompilerParams(collective_id=0, has_side_effects=True),
        name="request",
    )(ids, hidden)

    chunks = 4
    pieces = 4 if depth % 1024 == 0 else 1
    low, up, base, acc, stats, fresh = pl.pallas_call(
        functools.partial(local_kernel, groups, parts),
        out_shape=(
            shape((groups * rows, slot_rows), F32),
            shape((slot_rows, columns), BF16),
            shape((rows, kv_width), F32),
            shape((parts, here * rows, HD), BF16),
            shape((parts, 2 * rows, 128), F32),
            shape((rows, 128), F32),
        ),
        in_specs=[SMEM] * 3 + [VMEM] * 4 + [ANY] * 5,
        out_specs=(VMEM,) * 6,
        scratch_shapes=[
            pltpu.VMEM(cached_key_rows.shape, BF16),
            pltpu.VMEM(cached_value_rows.shape, BF16),
            pltpu.VMEM(value_projection_weight.shape, BF16),
            pltpu.VMEM((slot_rows, depth), BF16),
            pltpu.SMEM((groups * entries,), jnp.int32),
            dma((chunks,)),
            dma((chunks,)),
            dma((pieces,)),
            dma((groups * CAP,)),
            dma((groups * CAP,)),
        ],
        compiler_params=pltpu.CompilerParams(vmem_limit_bytes=32 * 1024 * 1024),
        name="local",
    )(
        ids_all,
        adapter_store_row,
        cache_length,
        hidden_all,
        hidden,
        query,
        new_token_keys,
        value_projection_weight,
        adapter_down_weight,
        adapter_up_weight,
        cached_key_rows,
        cached_value_rows,
    )

    return pl.pallas_call(
        functools.partial(finish_kernel, groups, parts),
        out_shape=(shape((rows, kv_width), BF16), shape((rows, here * HD), BF16)),
        in_specs=[VMEM] * 6,
        out_specs=(VMEM, VMEM),
        scratch_shapes=[
            pltpu.VMEM((parts, groups * rows, slot_rows), F32),
            pltpu.VMEM((parts, rows, kv_width), F32),
            pltpu.VMEM((parts, here * rows, HD), BF16),
            pltpu.VMEM((parts, 2 * rows, 128), F32),
            pltpu.VMEM((groups, rows, columns), F32),
            pltpu.VMEM((groups, parts, rows, columns), F32),
            pltpu.VMEM((kv_width // HD, rows, HD), F32),
            dma((4, parts)),
            dma((4, parts)),
            dma((total,)),
            dma((total,)),
        ],
        compiler_params=pltpu.CompilerParams(
            collective_id=1, has_side_effects=True, vmem_limit_bytes=32 * 1024 * 1024
        ),
        name="finish",
    )(low, up, base, acc, stats, fresh)


def solution(mesh):
    return jax.shard_map(
        functools.partial(per_device, mesh.shape["req"], mesh.shape["tp"]),
        mesh=mesh,
        in_specs=(
            P(("rep", "req"), "tp"),
            P("tp", None),
            P(("rep", "req"), None, "tp"),
            P(("rep", "req"), None, "tp"),
            P("rep"),
            P(("rep", "req")),
            P(("rep", "req"), None),
            P(("rep", "req")),
            P(("rep", "req"), None),
            P(("rep", "req"), "tp", None),
            P(("rep", "req"), "tp", None),
            P(("rep", "req"), None),
        ),
        out_specs=(P(("rep", "req"), None), P(("rep", "req"), "tp")),
        check_vma=False,
    )
```

```python
import functools

import jax
import jax.numpy as jnp
from jax import lax
from jax.experimental import pallas as pl
from jax.experimental.pallas import tpu as pltpu
from jax.sharding import PartitionSpec as P

HD = 128
ADAPTER_RANK = 16
CAP = 2
MASKED = -1e30
F32 = jnp.float32
BF16 = jnp.bfloat16
MESH = pl.DeviceIdType.MESH
VMEM = pl.BlockSpec(memory_space=pltpu.VMEM)
HBM = pl.BlockSpec(memory_space=pltpu.HBM)
ANY = pl.BlockSpec(memory_space=pl.ANY)
ROOM = 48 * 1024 * 1024


def dot_nt(a, b):
    return lax.dot_general(a, b, (((1,), (1,)), ((), ())), preferred_element_type=F32)


def repeated(x):
    for step in (16, 32, 64):
        x = x + pltpu.roll(x, step, axis=1)
    return x


def attend_kernel(
    groups,
    parts,
    wanted,
    picks,
    lengths,
    hidden,
    query,
    new_keys,
    keys,
    values,
    ids_out,
    hidden_out,
    acc_out,
    stats_out,
    fresh_out,
    wanted_s,
    picks_s,
    lengths_s,
    hidden_v,
    query_v,
    new_keys_v,
    key_buf,
    value_buf,
    acc_send,
    stats_send,
    small_sems,
    key_sems,
    value_sems,
    req_send,
    req_recv,
    tp_send,
    tp_recv,
):
    me = lax.axis_index("req")
    tp = lax.axis_index("tp")
    rows, depth = hidden.shape
    kv_width = new_keys.shape[1]
    kv_heads = kv_width // HD
    heads = query.shape[1] // HD
    per = heads // kv_heads
    here = heads // parts
    block = keys.shape[1]
    scale = HD ** (-0.5)
    half = depth // 2
    chunks = key_sems.shape[0]
    wide = kv_width // chunks
    inner = chunks == parts
    barrier = pltpu.get_barrier_semaphore()

    def greet_req(d, _):
        peer = lax.rem(me + d, groups)
        pl.semaphore_signal(barrier, inc=1, device_id={"req": peer}, device_id_type=MESH)
        return 0

    def greet_tp(d, _):
        peer = lax.rem(tp + d, parts)
        pl.semaphore_signal(barrier, inc=1, device_id={"tp": peer}, device_id_type=MESH)
        return 0

    lax.fori_loop(1, groups, greet_req, 0)
    lax.fori_loop(1, parts, greet_tp, 0)

    small = [
        pltpu.make_async_copy(source, landing, small_sems.at[n])
        for n, (source, landing) in enumerate(
            (
                (wanted, wanted_s),
                (picks, picks_s),
                (hidden, hidden_v),
                (lengths, lengths_s),
                (query, query_v),
                (new_keys, new_keys_v),
            )
        )
    ]
    for copy in small:
        copy.start()

    def cache_copies(d):
        chunk = lax.rem(tp + d, chunks) if inner else d
        part = pl.ds(pl.multiple_of(chunk * wide, HD), wide)
        return [
            pltpu.make_async_copy(source.at[:, :, part], landing.at[:, :, part], sems.at[chunk])
            for source, landing, sems in ((keys, key_buf, key_sems), (values, value_buf, value_sems))
        ]

    for d in range(1, chunks + 1):
        for copy in cache_copies(d if inner else d - 1):
            copy.start()

    for copy in small[:3]:
        copy.wait()
    wide_rows = hidden_v[...].astype(F32)
    hidden_out[me] = jnp.concatenate([wide_rows[:, :half], wide_rows[:, half:]], axis=0).astype(
        BF16
    )
    entries = wanted_s.shape[0]
    lane = lax.broadcasted_iota(jnp.int32, (entries, 128), 1)
    sub = lax.broadcasted_iota(jnp.int32, (entries, 128), 0)
    ids = jnp.zeros((entries, 128), jnp.int32)
    for e in range(entries):
        ids = jnp.where(sub == e, jnp.where(lane == 0, picks_s[e], wanted_s[e]), ids)
    ids_out[me] = ids
    pl.semaphore_wait(barrier, groups + parts - 2)

    def request(n, d):
        peer = lax.rem(me + d, groups)
        ref = (ids_out, hidden_out)[n]
        return pltpu.make_async_remote_copy(
            src_ref=ref.at[me],
            dst_ref=ref.at[me],
            send_sem=req_send.at[n, d],
            recv_sem=req_recv.at[n, d],
            device_id={"req": peer},
            device_id_type=MESH,
        )

    def share(n, d):
        peer = lax.rem(tp + d, parts)
        source, landing = ((acc_send, acc_out), (stats_send, stats_out))[n]
        return pltpu.make_async_remote_copy(
            src_ref=source.at[peer],
            dst_ref=landing.at[tp],
            send_sem=tp_send.at[n, d],
            recv_sem=tp_recv.at[n, d],
            device_id={"tp": peer},
            device_id_type=MESH,
        )

    def request_start(d, _):
        for n in range(2):
            request(n, d).start()
        return 0

    def request_wait(d, _):
        for n in range(2):
            request(n, d).wait()
        return 0

    def share_wait(d, _):
        for n in range(2):
            share(n, d).wait()
        return 0

    lax.fori_loop(1, groups, request_start, 0)
    for copy in small[3:]:
        copy.wait()

    count = min(per, here)
    spans = here // count
    tall = count * rows
    sub_b = lax.broadcasted_iota(jnp.int32, (rows, block), 0)
    length = jnp.zeros((rows, block), jnp.int32)
    for r in range(rows):
        length = jnp.where(sub_b == r, lengths_s[r], length)
    position = tp * block + lax.broadcasted_iota(jnp.int32, (rows, block), 1)
    valid = jnp.concatenate([(position < length).astype(jnp.int32)] * count, axis=0) > 0

    def own_row(width):
        row = lax.rem(lax.broadcasted_iota(jnp.int32, (tall, rows * width), 0), rows)
        col = lax.broadcasted_iota(jnp.int32, (tall, rows * width), 1) // width
        return jnp.where(row == col, 1.0, 0.0).astype(BF16)

    own_key = own_row(HD)
    lined = block % 128 == 0
    own_prob = own_key if block == HD else own_row(block) if lined else None
    row_of = lax.rem(lax.broadcasted_iota(jnp.int32, (tall, block), 0), rows)
    lane = lax.broadcasted_iota(jnp.int32, (rows, 128), 1)

    def columns(first):
        return pl.ds(pl.multiple_of(first * HD, HD), HD)

    def attend(d):
        peer = lax.rem(tp + d, parts)
        if inner:
            for copy in cache_copies(d):
                copy.wait()
        stats = jnp.zeros((rows, 128), F32)
        for i in range(spans):
            first = peer * here + i * count
            cols = columns(first // per)
            q = jnp.concatenate(
                [query_v[:, columns(first + g)].astype(F32) for g in range(count)], axis=0
            ).astype(BF16)
            q_wide = jnp.concatenate([q] * rows, axis=1) * own_key
            k_wide = jnp.concatenate([key_buf[r, :, cols] for r in range(rows)], axis=1)
            score = dot_nt(q_wide, k_wide) * scale
            score = jnp.where(valid, score, MASKED)
            peak = jnp.max(score, axis=1, keepdims=True)
            prob = jnp.where(valid, jnp.exp(score - peak), 0.0).astype(BF16)
            prob_f32 = prob.astype(F32)
            total = jnp.sum(prob_f32, axis=1, keepdims=True)
            if lined:
                p_wide = jnp.concatenate([prob] * rows, axis=1) * own_prob
                v_tall = value_buf[:, :, cols].reshape(rows * block, HD)
                acc = jnp.dot(p_wide, v_tall, preferred_element_type=F32)
            else:
                acc = jnp.zeros((tall, HD), F32)
                for r in range(rows):
                    p_row = jnp.where(row_of == r, prob_f32, 0.0).astype(BF16)
                    acc = acc + jnp.dot(p_row, value_buf[r, :, cols], preferred_element_type=F32)
            acc_send[peer, i * tall : (i + 1) * tall, :] = acc.astype(BF16)
            for g in range(count):
                part = slice(g * rows, (g + 1) * rows)
                stats = jnp.where(lane == i * count + g, peak[part], stats)
                stats = jnp.where(lane == 64 + i * count + g, total[part], stats)
        stats_send[peer] = stats

    if not inner:
        for d in range(chunks):
            for copy in cache_copies(d):
                copy.wait()

    def step(d, _):
        attend(d)
        for n in range(2):
            share(n, d).start()
        return 0

    lax.fori_loop(1, parts, step, 0)
    attend(parts)
    acc_out[tp] = acc_send[tp]
    stats_out[tp] = stats_send[tp]

    fresh = jnp.zeros((rows, 128), F32)
    for j in range(here):
        head = tp * here + j
        both = query_v[:, columns(head)].astype(F32) * new_keys_v[:, columns(head // per)].astype(
            F32
        )
        fresh = jnp.where(lane == j, jnp.sum(both, axis=1, keepdims=True) * scale, fresh)
    fresh_out[...] = fresh
    lax.fori_loop(1, groups, request_wait, 0)
    lax.fori_loop(1, parts, share_wait, 0)


def adapter_kernel(
    groups,
    parts,
    ids_in,
    hidden_all,
    table_in,
    weight,
    down,
    up,
    low_out,
    up_out,
    base_out,
    mask_out,
    ids,
    table,
    weight_buf,
    down_buf,
    slots,
    small_sems,
    weight_sems,
    down_sems,
    up_sems,
):
    me = lax.axis_index("req")
    depth, kv_width = weight.shape
    rows = hidden_all.shape[1] // 2
    store = down.shape[0]
    entries = ids.shape[1]
    columns = up.shape[2]
    half = depth // 2
    pieces = weight_sems.shape[0]
    tall = depth // pieces
    width = mask_out.shape[1]

    small = [
        pltpu.make_async_copy(ids_in, ids, small_sems.at[0]),
        pltpu.make_async_copy(table_in, table, small_sems.at[1]),
    ]

    def weight_copy(c):
        part = pl.ds(c * tall, tall)
        return pltpu.make_async_copy(weight.at[part, :], weight_buf.at[part, :], weight_sems.at[c])

    def down_copy(place, slot):
        part = pl.ds(slot * ADAPTER_RANK, ADAPTER_RANK)
        return pltpu.make_async_copy(down.at[place], down_buf.at[part, :], down_sems.at[slot])

    def up_copy(place, slot):
        part = pl.ds(lax.rem(slot, CAP) * ADAPTER_RANK, ADAPTER_RANK)
        return pltpu.make_async_copy(
            up.at[place], up_out.at[slot // CAP, part, :], up_sems.at[slot]
        )

    for copy in small:
        copy.start()
    for c in range(pieces):
        weight_copy(c).start()
    up_out[...] = jnp.zeros_like(up_out)
    for copy in small:
        copy.wait()

    counts = []
    for g in range(groups):
        count = jnp.int32(0)
        for e in range(entries):
            at = table[ids[g, e, 1]]
            mine = (at // store == me) & (count < CAP)
            slot = g * CAP + count
            slots[g * entries + e] = jnp.where(mine, slot, -1)

            @pl.when(mine)
            def _():
                down_copy(lax.rem(at, store), slot).start()
                up_copy(lax.rem(at, store), slot).start()

            count = count + mine.astype(jnp.int32)
        counts.append(count)

    owners = [table[ids[me, e, 1]] // store for e in range(entries)]
    for e in range(entries):
        order = jnp.int32(0)
        for before in range(e):
            order = order + (owners[before] == owners[e]).astype(jnp.int32)
        slots[groups * entries + e] = owners[e] * CAP + order
    slot_lane = lax.broadcasted_iota(jnp.int32, (rows, width), 1) // ADAPTER_RANK
    slot_row = lax.broadcasted_iota(jnp.int32, (rows, width), 0)
    place = jnp.full((rows, width), -1, jnp.int32)
    for r in range(rows):
        place = jnp.where(slot_row == r, slots[groups * entries + ids[me, r, 0]], place)
    mask_out[...] = jnp.where(place == slot_lane, 1.0, 0.0)

    own = hidden_all[me]
    base = [jnp.zeros((2 * rows, kv_width), F32) for _ in range(2)]
    for c in range(pieces):
        weight_copy(c).wait()
        side, at = divmod(c * tall, half)
        base[side] = base[side] + jnp.dot(
            own[:, at : at + tall], weight_buf[c * tall : (c + 1) * tall, :],
            preferred_element_type=F32,
        )
    both = base[0][:rows] + base[1][rows:]
    for p in range(parts):
        base_out[p] = both[:, p * columns : (p + 1) * columns]

    for g in range(groups):
        for c in range(CAP):

            @pl.when(counts[g] > c)
            def _():
                down_copy(0, g * CAP + c).wait()
                up_copy(0, g * CAP + c).wait()

    h_all = hidden_all[...].reshape(groups * 2 * rows, half)
    left = dot_nt(h_all, down_buf[:, :half])
    right = dot_nt(h_all, down_buf[:, half:])
    lane = lax.broadcasted_iota(jnp.int32, (rows, 128), 1) // ADAPTER_RANK
    sub = lax.broadcasted_iota(jnp.int32, (rows, 128), 0)
    for g in range(groups):
        wanted = jnp.full((rows, width), -1, jnp.int32)
        for r in range(rows):
            wanted = jnp.where(slot_row == r, slots[g * entries + ids[g, r, 0]], wanted)
        top = g * 2 * rows
        low = left[top : top + rows] + right[top + rows : top + 2 * rows]
        low = jnp.where(wanted == slot_lane, low, 0.0)
        folded = low[:, :128]
        for c in range(1, width // 128):
            folded = folded + low[:, c * 128 : (c + 1) * 128]
        low_out[g] = jnp.sum(
            jnp.where(lane == sub, repeated(folded), 0.0), axis=0, keepdims=True
        )


def finish_kernel(
    groups,
    parts,
    low,
    up,
    base,
    mask,
    acc,
    stats,
    fresh,
    value_out,
    attention_out,
    low_recv,
    up_recv,
    base_recv,
    value_recv,
    value_heads,
    low_send_sems,
    low_recv_sems,
    up_send_sems,
    up_recv_sems,
    tp_send_sems,
    tp_recv_sems,
):
    me = lax.axis_index("req")
    tp = lax.axis_index("tp")
    rows, kv_width = value_out.shape
    kv_heads = kv_width // HD
    here = attention_out.shape[1] // HD
    per = here * parts // kv_heads
    columns = up.shape[2]
    width = mask.shape[1]
    total = groups * parts
    mine = me * parts + tp
    barrier = pltpu.get_barrier_semaphore()

    def member(o):
        at = lax.rem(mine + o, total)
        return {"req": at // parts, "tp": lax.rem(at, parts)}

    def greet(o, _):
        pl.semaphore_signal(barrier, inc=1, device_id=member(o), device_id_type=MESH)
        return 0

    lax.fori_loop(1, total, greet, 0)
    low_recv[mine] = low[me]
    up_recv[me] = up[me]
    base_recv[tp] = base[tp]

    def low_copy(o):
        peer = member(o)
        return pltpu.make_async_remote_copy(
            src_ref=low.at[peer["req"]],
            dst_ref=low_recv.at[mine],
            send_sem=low_send_sems.at[o],
            recv_sem=low_recv_sems.at[o],
            device_id=peer,
            device_id_type=MESH,
        )

    def up_copy(d):
        peer = lax.rem(me + d, groups)
        return pltpu.make_async_remote_copy(
            src_ref=up.at[peer],
            dst_ref=up_recv.at[me],
            send_sem=up_send_sems.at[d],
            recv_sem=up_recv_sems.at[d],
            device_id={"req": peer},
            device_id_type=MESH,
        )

    def tp_copy(n, d):
        peer = lax.rem(tp + d, parts)
        source = value_recv.at[tp] if n else base.at[peer]
        landing = value_recv if n else base_recv
        return pltpu.make_async_remote_copy(
            src_ref=source,
            dst_ref=landing.at[tp],
            send_sem=tp_send_sems.at[n, d],
            recv_sem=tp_recv_sems.at[n, d],
            device_id={"tp": peer},
            device_id_type=MESH,
        )

    def each(count, act):
        def step(d, _):
            act(d)
            return 0

        lax.fori_loop(1, count, step, 0)

    pl.semaphore_wait(barrier, total - 1)
    each(parts, lambda d: tp_copy(0, d).start())
    each(groups, lambda d: up_copy(d).start())
    each(total, lambda o: low_copy(o).start())

    fresh_score = fresh[...]
    peak = fresh_score
    for p in range(parts):
        peak = jnp.maximum(peak, stats[p])
    fresh_weight = jnp.exp(fresh_score - peak)
    den = fresh_weight
    weights = []
    for p in range(parts):
        weight = jnp.exp(stats[p] - peak)
        den = den + weight * pltpu.roll(stats[p], 64, axis=1)
        weights.append(weight)
    inverse = 1.0 / den
    fresh_weight = fresh_weight * inverse
    weights = [weight * inverse for weight in weights]
    old = []
    for j in range(here):
        if (j * rows) % 16 == 0:
            pair = [acc[p, j * rows : (j + 2) * rows, :].astype(F32) for p in range(parts)]
        at = (j * rows) % 16
        part = jnp.zeros((rows, HD), F32)
        for p in range(parts):
            part = part + weights[p][:, j : j + 1] * pair[p][at : at + rows]
        old.append(part)

    each(parts, lambda d: tp_copy(0, d).wait_recv())
    base_sum = base_recv[0]
    for p in range(1, parts):
        base_sum = base_sum + base_recv[p]
    each(total, lambda o: low_copy(o).wait_recv())
    each(groups, lambda d: up_copy(d).wait_recv())
    rank_sum = jnp.sum(low_recv[...].reshape(total, 128), axis=0, keepdims=True)
    lane = lax.broadcasted_iota(jnp.int32, (rows, 128), 1) // ADAPTER_RANK
    sub = lax.broadcasted_iota(jnp.int32, (rows, 128), 0)
    by_row = repeated(jnp.where(lane == sub, jnp.broadcast_to(rank_sum, (rows, 128)), 0.0))
    low_rank = jnp.concatenate([by_row] * (width // 128), axis=1) * mask[...]
    coarse = low_rank.astype(BF16)
    fine = (low_rank - coarse.astype(F32)).astype(BF16)
    matrices = up_recv[...].reshape(width, columns)
    term = jnp.dot(coarse, matrices, preferred_element_type=F32) + jnp.dot(
        fine, matrices, preferred_element_type=F32
    )
    value_recv[tp] = (base_sum + term).astype(BF16).astype(F32)
    each(parts, lambda d: tp_copy(1, d).start())
    each(total, lambda o: low_copy(o).wait_send())
    each(groups, lambda d: up_copy(d).wait_send())
    each(parts, lambda d: tp_copy(0, d).wait_send())
    each(parts, lambda d: tp_copy(1, d).wait_recv())
    value = jnp.concatenate([value_recv[p] for p in range(parts)], axis=1)
    value_out[...] = value.astype(BF16)
    for k in range(kv_heads):
        value_heads[k] = value[:, k * HD : (k + 1) * HD]
    for j in range(here):
        fresh_value = value_heads[(tp * here + j) // per]
        out = old[j] + fresh_weight[:, j : j + 1] * fresh_value
        attention_out[:, j * HD : (j + 1) * HD] = out.astype(BF16)
    each(parts, lambda d: tp_copy(1, d).wait_send())


def per_device(
    groups,
    parts,
    hidden,
    value_projection_weight,
    adapter_down_weight,
    adapter_up_weight,
    adapter_store_row,
    request_group_adapters,
    row_list_entry,
    cache_length,
    query,
    cached_key_rows,
    cached_value_rows,
    new_token_keys,
):
    rows, depth = hidden.shape
    kv_width = new_token_keys.shape[1]
    kv_heads = kv_width // HD
    columns = adapter_up_weight.shape[2]
    heads = query.shape[1] // HD
    here = heads // parts
    entries = request_group_adapters.shape[0]
    slot_rows = groups * CAP * ADAPTER_RANK
    total = groups * parts
    chunks = min(parts, kv_heads)
    dma = pltpu.SemaphoreType.DMA
    shape = jax.ShapeDtypeStruct

    ids_all, hidden_all, acc, stats, fresh = pl.pallas_call(
        functools.partial(attend_kernel, groups, parts),
        out_shape=(
            shape((groups, entries, 128), jnp.int32),
            shape((groups, 2 * rows, depth // 2), BF16),
            shape((parts, here * rows, HD), BF16),
            shape((parts, rows, 128), F32),
            shape((rows, 128), F32),
        ),
        in_specs=[HBM] * 8,
        out_specs=(VMEM,) * 5,
        scratch_shapes=[
            pltpu.SMEM((entries,), jnp.int32),
            pltpu.SMEM((rows,), jnp.int32),
            pltpu.SMEM((rows,), jnp.int32),
            pltpu.VMEM(hidden.shape, BF16),
            pltpu.VMEM(query.shape, BF16),
            pltpu.VMEM(new_token_keys.shape, BF16),
            pltpu.VMEM(cached_key_rows.shape, BF16),
            pltpu.VMEM(cached_value_rows.shape, BF16),
            pltpu.VMEM((parts, here * rows, HD), BF16),
            pltpu.VMEM((parts, rows, 128), F32),
            dma((6,)),
            dma((chunks,)),
            dma((chunks,)),
            dma((2, groups)),
            dma((2, groups)),
            dma((2, parts)),
            dma((2, parts)),
        ],
        compiler_params=pltpu.CompilerParams(
            collective_id=0, has_side_effects=True, vmem_limit_bytes=ROOM
        ),
        name="attend",
    )(
        request_group_adapters,
        row_list_entry.reshape(rows),
        cache_length,
        hidden,
        query,
        new_token_keys,
        cached_key_rows,
        cached_value_rows,
    )

    pieces = 4 if depth % 1024 == 0 else 2
    low, up, base, mask = pl.pallas_call(
        functools.partial(adapter_kernel, groups, parts),
        out_shape=(
            shape((groups, 1, 128), F32),
            shape((groups, CAP * ADAPTER_RANK, columns), BF16),
            shape((parts, rows, columns), F32),
            shape((rows, slot_rows), F32),
        ),
        in_specs=[ANY, VMEM] + [HBM] * 4,
        out_specs=(VMEM,) * 4,
        scratch_shapes=[
            pltpu.SMEM((groups, entries, 128), jnp.int32),
            pltpu.SMEM(adapter_store_row.shape, jnp.int32),
            pltpu.VMEM(value_projection_weight.shape, BF16),
            pltpu.VMEM((slot_rows, depth), BF16),
            pltpu.SMEM(((groups + 1) * entries,), jnp.int32),
            dma((2,)),
            dma((pieces,)),
            dma((groups * CAP,)),
            dma((groups * CAP,)),
        ],
        compiler_params=pltpu.CompilerParams(vmem_limit_bytes=ROOM),
        name="adapters",
    )(
        ids_all,
        hidden_all,
        adapter_store_row,
        value_projection_weight,
        adapter_down_weight,
        adapter_up_weight,
    )

    return pl.pallas_call(
        functools.partial(finish_kernel, groups, parts),
        out_shape=(shape((rows, kv_width), BF16), shape((rows, here * HD), BF16)),
        in_specs=[VMEM] * 7,
        out_specs=(VMEM, VMEM),
        scratch_shapes=[
            pltpu.VMEM((total, 1, 128), F32),
            pltpu.VMEM((groups, CAP * ADAPTER_RANK, columns), BF16),
            pltpu.VMEM((parts, rows, columns), F32),
            pltpu.VMEM((parts, rows, columns), F32),
            pltpu.VMEM((kv_heads, rows, HD), F32),
            dma((total,)),
            dma((total,)),
            dma((groups,)),
            dma((groups,)),
            dma((2, parts)),
            dma((2, parts)),
        ],
        compiler_params=pltpu.CompilerParams(
            collective_id=1, has_side_effects=True, vmem_limit_bytes=ROOM
        ),
        name="finish",
    )(low, up, base, mask, acc, stats, fresh)


def solution(mesh):
    return jax.shard_map(
        functools.partial(per_device, mesh.shape["req"], mesh.shape["tp"]),
        mesh=mesh,
        in_specs=(
            P(("rep", "req"), "tp"),
            P("tp", None),
            P(("rep", "req"), None, "tp"),
            P(("rep", "req"), None, "tp"),
            P("rep"),
            P(("rep", "req")),
            P(("rep", "req"), None),
            P(("rep", "req")),
            P(("rep", "req"), None),
            P(("rep", "req"), "tp", None),
            P(("rep", "req"), "tp", None),
            P(("rep", "req"), None),
        ),
        out_specs=(P(("rep", "req"), None), P(("rep", "req"), "tp")),
        check_vma=False,
    )
```

```python
import functools

import jax
import jax.numpy as jnp
from jax import lax
from jax.experimental import pallas as pl
from jax.experimental.pallas import tpu as pltpu
from jax.sharding import PartitionSpec as P

HD = 128
ADAPTER_RANK = 16
CAP = 2
MASKED = -1e30
F32 = jnp.float32
BF16 = jnp.bfloat16
MESH = pl.DeviceIdType.MESH
VMEM = pl.BlockSpec(memory_space=pltpu.VMEM)
ANY = pl.BlockSpec(memory_space=pl.ANY)
ROOM = 60 * 1024 * 1024


def dot_nt(a, b):
    return lax.dot_general(a, b, (((1,), (1,)), ((), ())), preferred_element_type=F32)


def repeated(x):
    for step in (16, 32, 64):
        x = x + pltpu.roll(x, step, axis=1)
    return x


def attend_kernel(
    groups,
    parts,
    wanted,
    picks,
    lengths,
    hidden,
    query,
    new_keys,
    keys,
    values,
    weight,
    ids_out,
    hidden_out,
    acc_out,
    stats_out,
    fresh_out,
    base_out,
    wanted_s,
    picks_s,
    lengths_s,
    hidden_v,
    query_v,
    new_keys_v,
    key_buf,
    value_buf,
    weight_buf,
    ids_v,
    packed_v,
    acc_send,
    stats_send,
    fresh_v,
    base_v,
    small_sems,
    key_sems,
    value_sems,
    weight_sems,
    own_sems,
    req_send,
    req_recv,
    tp_send,
    tp_recv,
):
    me = lax.axis_index("req")
    tp = lax.axis_index("tp")
    rows, depth = hidden.shape
    kv_width = new_keys.shape[1]
    kv_heads = kv_width // HD
    heads = query.shape[1] // HD
    per = heads // kv_heads
    here = heads // parts
    block = keys.shape[1]
    scale = HD ** (-0.5)
    half = depth // 2
    chunks = key_sems.shape[0]
    wide = kv_width // chunks
    inner = chunks == parts
    barrier = pltpu.get_barrier_semaphore()

    def greet_req(d, _):
        peer = lax.rem(me + d, groups)
        pl.semaphore_signal(barrier, inc=1, device_id={"req": peer}, device_id_type=MESH)
        return 0

    def greet_tp(d, _):
        peer = lax.rem(tp + d, parts)
        pl.semaphore_signal(barrier, inc=1, device_id={"tp": peer}, device_id_type=MESH)
        return 0

    lax.fori_loop(1, groups, greet_req, 0)
    lax.fori_loop(1, parts, greet_tp, 0)

    small = [
        pltpu.make_async_copy(source, landing, small_sems.at[n])
        for n, (source, landing) in enumerate(
            (
                (wanted, wanted_s),
                (picks, picks_s),
                (hidden, hidden_v),
                (lengths, lengths_s),
                (query, query_v),
                (new_keys, new_keys_v),
            )
        )
    ]
    for copy in small:
        copy.start()

    def cache_copies(d):
        chunk = lax.rem(tp + d, chunks) if inner else d
        part = pl.ds(pl.multiple_of(chunk * wide, HD), wide)
        return [
            pltpu.make_async_copy(source.at[:, :, part], landing.at[:, :, part], sems.at[chunk])
            for source, landing, sems in ((keys, key_buf, key_sems), (values, value_buf, value_sems))
        ]

    for d in range(1, chunks + 1):
        for copy in cache_copies(d if inner else d - 1):
            copy.start()

    pieces = weight_sems.shape[0]
    deep = depth // pieces

    def weight_copy(c):
        part = pl.ds(c * deep, deep)
        return pltpu.make_async_copy(weight.at[part, :], weight_buf.at[part, :], weight_sems.at[c])

    for c in range(pieces):
        weight_copy(c).start()
    own = [
        pltpu.make_async_copy(source, landing, own_sems.at[n])
        for n, (source, landing) in enumerate(
            (
                (ids_v, ids_out.at[me]),
                (packed_v, hidden_out.at[me]),
                (acc_send.at[tp], acc_out.at[tp]),
                (stats_send.at[tp], stats_out.at[tp]),
                (fresh_v, fresh_out),
                (base_v, base_out),
            )
        )
    ]

    for copy in small[:3]:
        copy.wait()
    wide_rows = hidden_v[...].astype(F32)
    packed_v[...] = jnp.concatenate([wide_rows[:, :half], wide_rows[:, half:]], axis=0).astype(BF16)
    entries = wanted_s.shape[0]
    lane = lax.broadcasted_iota(jnp.int32, (entries, 128), 1)
    sub = lax.broadcasted_iota(jnp.int32, (entries, 128), 0)
    ids = jnp.zeros((entries, 128), jnp.int32)
    for e in range(entries):
        ids = jnp.where(sub == e, jnp.where(lane == 0, picks_s[e], wanted_s[e]), ids)
    ids_v[...] = ids
    for copy in own[:2]:
        copy.start()
    pl.semaphore_wait(barrier, groups + parts - 2)

    def request(n, d):
        peer = lax.rem(me + d, groups)
        source, landing = ((ids_v, ids_out), (packed_v, hidden_out))[n]
        return pltpu.make_async_remote_copy(
            src_ref=source,
            dst_ref=landing.at[me],
            send_sem=req_send.at[n, d],
            recv_sem=req_recv.at[n, d],
            device_id={"req": peer},
            device_id_type=MESH,
        )

    def share(n, d):
        peer = lax.rem(tp + d, parts)
        source, landing = ((acc_send, acc_out), (stats_send, stats_out))[n]
        return pltpu.make_async_remote_copy(
            src_ref=source.at[peer],
            dst_ref=landing.at[tp],
            send_sem=tp_send.at[n, d],
            recv_sem=tp_recv.at[n, d],
            device_id={"tp": peer},
            device_id_type=MESH,
        )

    def request_start(d, _):
        for n in range(2):
            request(n, d).start()
        return 0

    def request_wait(d, _):
        for n in range(2):
            request(n, d).wait()
        return 0

    def share_wait(d, _):
        for n in range(2):
            share(n, d).wait()
        return 0

    lax.fori_loop(1, groups, request_start, 0)
    for copy in small[3:]:
        copy.wait()

    count = min(per, here)
    spans = here // count
    tall = count * rows
    sub_b = lax.broadcasted_iota(jnp.int32, (rows, block), 0)
    length = jnp.zeros((rows, block), jnp.int32)
    for r in range(rows):
        length = jnp.where(sub_b == r, lengths_s[r], length)
    position = tp * block + lax.broadcasted_iota(jnp.int32, (rows, block), 1)
    valid = jnp.concatenate([(position < length).astype(jnp.int32)] * count, axis=0) > 0

    def own_row(width):
        row = lax.rem(lax.broadcasted_iota(jnp.int32, (tall, rows * width), 0), rows)
        col = lax.broadcasted_iota(jnp.int32, (tall, rows * width), 1) // width
        return jnp.where(row == col, 1.0, 0.0).astype(BF16)

    own_key = own_row(HD)
    lined = block % 128 == 0
    own_prob = own_key if block == HD else own_row(block) if lined else None
    row_of = lax.rem(lax.broadcasted_iota(jnp.int32, (tall, block), 0), rows)
    lane = lax.broadcasted_iota(jnp.int32, (rows, 128), 1)

    def columns(first):
        return pl.ds(pl.multiple_of(first * HD, HD), HD)

    def attend(d):
        peer = lax.rem(tp + d, parts)
        if inner:
            for copy in cache_copies(d):
                copy.wait()
        stats = jnp.zeros((rows, 128), F32)
        for i in range(spans):
            first = peer * here + i * count
            cols = columns(first // per)
            q = jnp.concatenate(
                [query_v[:, columns(first + g)].astype(F32) for g in range(count)], axis=0
            ).astype(BF16)
            q_wide = jnp.concatenate([q] * rows, axis=1) * own_key
            k_wide = jnp.concatenate([key_buf[r, :, cols] for r in range(rows)], axis=1)
            score = dot_nt(q_wide, k_wide) * scale
            score = jnp.where(valid, score, MASKED)
            peak = jnp.max(score, axis=1, keepdims=True)
            prob = jnp.where(valid, jnp.exp(score - peak), 0.0).astype(BF16)
            prob_f32 = prob.astype(F32)
            total = jnp.sum(prob_f32, axis=1, keepdims=True)
            if lined:
                p_wide = jnp.concatenate([prob] * rows, axis=1) * own_prob
                v_tall = value_buf[:, :, cols].reshape(rows * block, HD)
                acc = jnp.dot(p_wide, v_tall, preferred_element_type=F32)
            else:
                acc = jnp.zeros((tall, HD), F32)
                for r in range(rows):
                    p_row = jnp.where(row_of == r, prob_f32, 0.0).astype(BF16)
                    acc = acc + jnp.dot(p_row, value_buf[r, :, cols], preferred_element_type=F32)
            acc_send[peer, i * tall : (i + 1) * tall, :] = acc.astype(BF16)
            for g in range(count):
                part = slice(g * rows, (g + 1) * rows)
                stats = jnp.where(lane == i * count + g, peak[part], stats)
                stats = jnp.where(lane == 64 + i * count + g, total[part], stats)
        stats_send[peer] = stats

    if not inner:
        for d in range(chunks):
            for copy in cache_copies(d):
                copy.wait()

    def step(d, _):
        attend(d)
        for n in range(2):
            share(n, d).start()
        return 0

    lax.fori_loop(1, parts, step, 0)
    attend(parts)
    for copy in own[2:4]:
        copy.start()

    fresh = jnp.zeros((rows, 128), F32)
    for j in range(here):
        head = tp * here + j
        both = query_v[:, columns(head)].astype(F32) * new_keys_v[:, columns(head // per)].astype(
            F32
        )
        fresh = jnp.where(lane == j, jnp.sum(both, axis=1, keepdims=True) * scale, fresh)
    fresh_v[...] = fresh
    own[4].start()
    base = jnp.zeros((rows, kv_width), F32)
    for c in range(pieces):
        weight_copy(c).wait()
        part = slice(c * deep, (c + 1) * deep)
        base = base + jnp.dot(hidden_v[:, part], weight_buf[part, :], preferred_element_type=F32)
    share_cols = base_v.shape[2]
    for p in range(parts):
        base_v[p] = base[:, p * share_cols : (p + 1) * share_cols]
    own[5].start()
    lax.fori_loop(1, groups, request_wait, 0)
    lax.fori_loop(1, parts, share_wait, 0)
    for copy in own:
        copy.wait()


def adapter_kernel(
    groups,
    parts,
    ids_in,
    hidden_in,
    table_in,
    down,
    up,
    low_out,
    up_out,
    mask_out,
    ids,
    table,
    hidden_all,
    down_buf,
    low_v,
    up_v,
    mask_v,
    slots,
    small_sems,
    down_sems,
    up_sems,
):
    me = lax.axis_index("req")
    depth = down.shape[2]
    rows = hidden_all.shape[1] // 2
    store = down.shape[0]
    entries = ids.shape[1]
    half = depth // 2
    width = mask_out.shape[1]

    small = [
        pltpu.make_async_copy(ids_in, ids, small_sems.at[0]),
        pltpu.make_async_copy(table_in, table, small_sems.at[1]),
        pltpu.make_async_copy(hidden_in, hidden_all, small_sems.at[2]),
    ]
    results = [
        pltpu.make_async_copy(source, landing, small_sems.at[3 + n])
        for n, (source, landing) in enumerate(((low_v, low_out), (up_v, up_out), (mask_v, mask_out)))
    ]

    def down_copy(place, slot):
        part = pl.ds(slot * ADAPTER_RANK, ADAPTER_RANK)
        return pltpu.make_async_copy(down.at[place], down_buf.at[part, :], down_sems.at[slot])

    def up_copy(place, slot):
        part = pl.ds(lax.rem(slot, CAP) * ADAPTER_RANK, ADAPTER_RANK)
        return pltpu.make_async_copy(
            up.at[place], up_v.at[slot // CAP, part, :], up_sems.at[slot]
        )

    for copy in small:
        copy.start()
    up_v[...] = jnp.zeros_like(up_v)
    for copy in small[:2]:
        copy.wait()

    counts = []
    for g in range(groups):
        count = jnp.int32(0)
        for e in range(entries):
            at = table[ids[g, e, 1]]
            mine = (at // store == me) & (count < CAP)
            slot = g * CAP + count
            slots[g * entries + e] = jnp.where(mine, slot, -1)

            @pl.when(mine)
            def _():
                down_copy(lax.rem(at, store), slot).start()
                up_copy(lax.rem(at, store), slot).start()

            count = count + mine.astype(jnp.int32)
        counts.append(count)

    owners = [table[ids[me, e, 1]] // store for e in range(entries)]
    for e in range(entries):
        order = jnp.int32(0)
        for before in range(e):
            order = order + (owners[before] == owners[e]).astype(jnp.int32)
        slots[groups * entries + e] = owners[e] * CAP + order
    slot_lane = lax.broadcasted_iota(jnp.int32, (rows, width), 1) // ADAPTER_RANK
    slot_row = lax.broadcasted_iota(jnp.int32, (rows, width), 0)
    place = jnp.full((rows, width), -1, jnp.int32)
    for r in range(rows):
        place = jnp.where(slot_row == r, slots[groups * entries + ids[me, r, 0]], place)
    mask_v[...] = jnp.where(place == slot_lane, 1.0, 0.0)
    results[2].start()

    for g in range(groups):
        for c in range(CAP):

            @pl.when(counts[g] > c)
            def _():
                down_copy(0, g * CAP + c).wait()
                up_copy(0, g * CAP + c).wait()

    results[1].start()
    small[2].wait()
    h_all = hidden_all[...].reshape(groups * 2 * rows, half)
    left = dot_nt(h_all, down_buf[:, :half])
    right = dot_nt(h_all, down_buf[:, half:])
    lane = lax.broadcasted_iota(jnp.int32, (rows, 128), 1) // ADAPTER_RANK
    sub = lax.broadcasted_iota(jnp.int32, (rows, 128), 0)
    for g in range(groups):
        wanted = jnp.full((rows, width), -1, jnp.int32)
        for r in range(rows):
            wanted = jnp.where(slot_row == r, slots[g * entries + ids[g, r, 0]], wanted)
        top = g * 2 * rows
        low = left[top : top + rows] + right[top + rows : top + 2 * rows]
        low = jnp.where(wanted == slot_lane, low, 0.0)
        folded = low[:, :128]
        for c in range(1, width // 128):
            folded = folded + low[:, c * 128 : (c + 1) * 128]
        low_v[g] = jnp.sum(jnp.where(lane == sub, repeated(folded), 0.0), axis=0, keepdims=True)
    results[0].start()
    for copy in results:
        copy.wait()


def finish_kernel(
    groups,
    parts,
    low,
    up,
    base,
    mask,
    acc,
    stats,
    fresh,
    value_out,
    attention_out,
    low_recv,
    up_recv,
    base_recv,
    value_recv,
    value_heads,
    mask_v,
    acc_v,
    stats_v,
    fresh_v,
    own_sems,
    low_send_sems,
    low_recv_sems,
    up_send_sems,
    up_recv_sems,
    tp_send_sems,
    tp_recv_sems,
):
    me = lax.axis_index("req")
    tp = lax.axis_index("tp")
    rows, kv_width = value_out.shape
    kv_heads = kv_width // HD
    here = attention_out.shape[1] // HD
    per = here * parts // kv_heads
    columns = up.shape[2]
    width = mask.shape[1]
    total = groups * parts
    mine = me * parts + tp
    barrier = pltpu.get_barrier_semaphore()

    def member(o):
        at = lax.rem(mine + o, total)
        return {"req": at // parts, "tp": lax.rem(at, parts)}

    def greet(o, _):
        pl.semaphore_signal(barrier, inc=1, device_id=member(o), device_id_type=MESH)
        return 0

    lax.fori_loop(1, total, greet, 0)
    own = [
        pltpu.make_async_copy(source, landing, own_sems.at[n])
        for n, (source, landing) in enumerate(
            (
                (stats, stats_v),
                (fresh, fresh_v),
                (acc, acc_v),
                (base.at[tp], base_recv.at[tp]),
                (low.at[me], low_recv.at[mine]),
                (up.at[me], up_recv.at[me]),
                (mask, mask_v),
            )
        )
    ]
    for copy in own:
        copy.start()

    def low_copy(o):
        peer = member(o)
        return pltpu.make_async_remote_copy(
            src_ref=low.at[peer["req"]],
            dst_ref=low_recv.at[mine],
            send_sem=low_send_sems.at[o],
            recv_sem=low_recv_sems.at[o],
            device_id=peer,
            device_id_type=MESH,
        )

    def up_copy(d):
        peer = lax.rem(me + d, groups)
        return pltpu.make_async_remote_copy(
            src_ref=up.at[peer],
            dst_ref=up_recv.at[me],
            send_sem=up_send_sems.at[d],
            recv_sem=up_recv_sems.at[d],
            device_id={"req": peer},
            device_id_type=MESH,
        )

    def tp_copy(n, d):
        peer = lax.rem(tp + d, parts)
        source = value_recv.at[tp] if n else base.at[peer]
        landing = value_recv if n else base_recv
        return pltpu.make_async_remote_copy(
            src_ref=source,
            dst_ref=landing.at[tp],
            send_sem=tp_send_sems.at[n, d],
            recv_sem=tp_recv_sems.at[n, d],
            device_id={"tp": peer},
            device_id_type=MESH,
        )

    def each(count, act):
        def step(d, _):
            act(d)
            return 0

        lax.fori_loop(1, count, step, 0)

    pl.semaphore_wait(barrier, total - 1)
    each(parts, lambda d: tp_copy(0, d).start())
    each(groups, lambda d: up_copy(d).start())
    each(total, lambda o: low_copy(o).start())

    for copy in own[:3]:
        copy.wait()
    fresh_score = fresh_v[...]
    peak = fresh_score
    for p in range(parts):
        peak = jnp.maximum(peak, stats_v[p])
    fresh_weight = jnp.exp(fresh_score - peak)
    den = fresh_weight
    weights = []
    for p in range(parts):
        weight = jnp.exp(stats_v[p] - peak)
        den = den + weight * pltpu.roll(stats_v[p], 64, axis=1)
        weights.append(weight)
    inverse = 1.0 / den
    fresh_weight = fresh_weight * inverse
    weights = [weight * inverse for weight in weights]
    old = []
    for j in range(here):
        if (j * rows) % 16 == 0:
            pair = [acc_v[p, j * rows : (j + 2) * rows, :].astype(F32) for p in range(parts)]
        at = (j * rows) % 16
        part = jnp.zeros((rows, HD), F32)
        for p in range(parts):
            part = part + weights[p][:, j : j + 1] * pair[p][at : at + rows]
        old.append(part)

    for copy in own[3:]:
        copy.wait()
    each(parts, lambda d: tp_copy(0, d).wait_recv())
    base_sum = base_recv[0]
    for p in range(1, parts):
        base_sum = base_sum + base_recv[p]
    each(total, lambda o: low_copy(o).wait_recv())
    each(groups, lambda d: up_copy(d).wait_recv())
    rank_sum = jnp.sum(low_recv[...].reshape(total, 128), axis=0, keepdims=True)
    lane = lax.broadcasted_iota(jnp.int32, (rows, 128), 1) // ADAPTER_RANK
    sub = lax.broadcasted_iota(jnp.int32, (rows, 128), 0)
    by_row = repeated(jnp.where(lane == sub, jnp.broadcast_to(rank_sum, (rows, 128)), 0.0))
    low_rank = jnp.concatenate([by_row] * (width // 128), axis=1) * mask_v[...]
    coarse = low_rank.astype(BF16)
    fine = (low_rank - coarse.astype(F32)).astype(BF16)
    matrices = up_recv[...].reshape(width, columns)
    term = jnp.dot(coarse, matrices, preferred_element_type=F32) + jnp.dot(
        fine, matrices, preferred_element_type=F32
    )
    value_recv[tp] = (base_sum + term).astype(BF16).astype(F32)
    each(parts, lambda d: tp_copy(1, d).start())
    each(total, lambda o: low_copy(o).wait_send())
    each(groups, lambda d: up_copy(d).wait_send())
    each(parts, lambda d: tp_copy(0, d).wait_send())
    each(parts, lambda d: tp_copy(1, d).wait_recv())
    value = jnp.concatenate([value_recv[p] for p in range(parts)], axis=1)
    value_out[...] = value.astype(BF16)
    for k in range(kv_heads):
        value_heads[k] = value[:, k * HD : (k + 1) * HD]
    for j in range(here):
        fresh_value = value_heads[(tp * here + j) // per]
        out = old[j] + fresh_weight[:, j : j + 1] * fresh_value
        attention_out[:, j * HD : (j + 1) * HD] = out.astype(BF16)
    each(parts, lambda d: tp_copy(1, d).wait_send())


def per_device(
    groups,
    parts,
    hidden,
    value_projection_weight,
    adapter_down_weight,
    adapter_up_weight,
    adapter_store_row,
    request_group_adapters,
    row_list_entry,
    cache_length,
    query,
    cached_key_rows,
    cached_value_rows,
    new_token_keys,
):
    rows, depth = hidden.shape
    kv_width = new_token_keys.shape[1]
    kv_heads = kv_width // HD
    columns = adapter_up_weight.shape[2]
    heads = query.shape[1] // HD
    here = heads // parts
    entries = request_group_adapters.shape[0]
    slot_rows = groups * CAP * ADAPTER_RANK
    total = groups * parts
    chunks = min(parts, kv_heads)
    dma = pltpu.SemaphoreType.DMA
    shape = jax.ShapeDtypeStruct

    pieces = 4 if depth % 1024 == 0 else 2
    ids_all, hidden_all, acc, stats, fresh, base = pl.pallas_call(
        functools.partial(attend_kernel, groups, parts),
        out_shape=(
            shape((groups, entries, 128), jnp.int32),
            shape((groups, 2 * rows, depth // 2), BF16),
            shape((parts, here * rows, HD), BF16),
            shape((parts, rows, 128), F32),
            shape((rows, 128), F32),
            shape((parts, rows, columns), F32),
        ),
        in_specs=[ANY] * 9,
        out_specs=(ANY,) * 6,
        scratch_shapes=[
            pltpu.SMEM((entries,), jnp.int32),
            pltpu.SMEM((rows,), jnp.int32),
            pltpu.SMEM((rows,), jnp.int32),
            pltpu.VMEM(hidden.shape, BF16),
            pltpu.VMEM(query.shape, BF16),
            pltpu.VMEM(new_token_keys.shape, BF16),
            pltpu.VMEM(cached_key_rows.shape, BF16),
            pltpu.VMEM(cached_value_rows.shape, BF16),
            pltpu.VMEM(value_projection_weight.shape, BF16),
            pltpu.VMEM((entries, 128), jnp.int32),
            pltpu.VMEM((2 * rows, depth // 2), BF16),
            pltpu.VMEM((parts, here * rows, HD), BF16),
            pltpu.VMEM((parts, rows, 128), F32),
            pltpu.VMEM((rows, 128), F32),
            pltpu.VMEM((parts, rows, columns), F32),
            dma((6,)),
            dma((chunks,)),
            dma((chunks,)),
            dma((pieces,)),
            dma((6,)),
            dma((2, groups)),
            dma((2, groups)),
            dma((2, parts)),
            dma((2, parts)),
        ],
        compiler_params=pltpu.CompilerParams(
            collective_id=0, has_side_effects=True, vmem_limit_bytes=ROOM
        ),
        name="attend",
    )(
        request_group_adapters,
        row_list_entry.reshape(rows),
        cache_length,
        hidden,
        query,
        new_token_keys,
        cached_key_rows,
        cached_value_rows,
        value_projection_weight,
    )

    low, up, mask = pl.pallas_call(
        functools.partial(adapter_kernel, groups, parts),
        out_shape=(
            shape((groups, 1, 128), F32),
            shape((groups, CAP * ADAPTER_RANK, columns), BF16),
            shape((rows, slot_rows), F32),
        ),
        in_specs=[ANY] * 5,
        out_specs=(ANY,) * 3,
        scratch_shapes=[
            pltpu.SMEM((groups, entries, 128), jnp.int32),
            pltpu.SMEM(adapter_store_row.shape, jnp.int32),
            pltpu.VMEM((groups, 2 * rows, depth // 2), BF16),
            pltpu.VMEM((slot_rows, depth), BF16),
            pltpu.VMEM((groups, 1, 128), F32),
            pltpu.VMEM((groups, CAP * ADAPTER_RANK, columns), BF16),
            pltpu.VMEM((rows, slot_rows), F32),
            pltpu.SMEM(((groups + 1) * entries,), jnp.int32),
            dma((6,)),
            dma((groups * CAP,)),
            dma((groups * CAP,)),
        ],
        compiler_params=pltpu.CompilerParams(vmem_limit_bytes=ROOM),
        name="adapters",
    )(
        ids_all,
        hidden_all,
        adapter_store_row,
        adapter_down_weight,
        adapter_up_weight,
    )

    return pl.pallas_call(
        functools.partial(finish_kernel, groups, parts),
        out_shape=(shape((rows, kv_width), BF16), shape((rows, here * HD), BF16)),
        in_specs=[ANY] * 7,
        out_specs=(VMEM, VMEM),
        scratch_shapes=[
            pltpu.VMEM((total, 1, 128), F32),
            pltpu.VMEM((groups, CAP * ADAPTER_RANK, columns), BF16),
            pltpu.VMEM((parts, rows, columns), F32),
            pltpu.VMEM((parts, rows, columns), F32),
            pltpu.VMEM((kv_heads, rows, HD), F32),
            pltpu.VMEM(mask.shape, F32),
            pltpu.VMEM(acc.shape, BF16),
            pltpu.VMEM(stats.shape, F32),
            pltpu.VMEM(fresh.shape, F32),
            dma((7,)),
            dma((total,)),
            dma((total,)),
            dma((groups,)),
            dma((groups,)),
            dma((2, parts)),
            dma((2, parts)),
        ],
        compiler_params=pltpu.CompilerParams(
            collective_id=1, has_side_effects=True, vmem_limit_bytes=ROOM
        ),
        name="finish",
    )(low, up, base, mask, acc, stats, fresh)


def solution(mesh):
    return jax.shard_map(
        functools.partial(per_device, mesh.shape["req"], mesh.shape["tp"]),
        mesh=mesh,
        in_specs=(
            P(("rep", "req"), "tp"),
            P("tp", None),
            P(("rep", "req"), None, "tp"),
            P(("rep", "req"), None, "tp"),
            P("rep"),
            P(("rep", "req")),
            P(("rep", "req"), None),
            P(("rep", "req")),
            P(("rep", "req"), None),
            P(("rep", "req"), "tp", None),
            P(("rep", "req"), "tp", None),
            P(("rep", "req"), None),
        ),
        out_specs=(P(("rep", "req"), None), P(("rep", "req"), "tp")),
        check_vma=False,
    )
```
